32 devices in a mesh: dp: 8 (over z, x), tensor: 4 (over y, core).
Axes of the slice: x: 2, y: 2, z: 4, core: 2. Of those that a mesh axis runs over, the one named last changes fastest.
Arguments:
- tokens: bfloat16 [2048, 1024], P('dp'), may hold values from -6 to 6
- cotangent: bfloat16 [2048, 1024], P('dp'), may hold values from -6 to 6
- seq_lengths: int32 [8, 3], P('dp'), may hold values from 1 to 224, 256 in all within a row
- routes: int32 [2048, 8], P('dp'), may hold values from 0 to 31, all different within a row; in each aligned block of 256 rows (0 to 255, 256 to 511, ...) at most 80 rows name the same one
- gates: float32 [2048, 8], P('dp'), may hold values from 0 to 1, as said below
- norm1_gain: float32 [1024], replicated, may hold values from 0.5 to 1.5
- w_query: bfloat16 [1024, 1024], P(None, 'tensor'), may hold values from -0.1875 to 0.1875
- key_weight: bfloat16 [1024, 512], P(None, 'tensor'), may hold values from -0.1875 to 0.1875
- value_weight: bfloat16 [1024, 512], P(None, 'tensor'), may hold values from -0.1875 to 0.1875
- w_output: bfloat16 [1024, 1024], P('tensor'), may hold values from -0.75 to 0.75
- norm2_gain: float32 [1024], replicated, may hold values from 0.5 to 1.5
- w_gate: bfloat16 [32, 1024, 512], P('dp', None, 'tensor'), may hold values from -0.1875 to 0.1875
- w_up: bfloat16 [32, 1024, 512], P('dp', None, 'tensor'), may hold values from -0.1875 to 0.1875
- w_down: bfloat16 [32, 512, 1024], P('dp', 'tensor'), may hold values from -1 to 1
Outputs:
- layer_out: bfloat16 [2048, 1024], P('dp')
- d_tokens: float32 [2048, 1024], P('dp')
- d_norm1_gain: float32 [1024], replicated
- d_w_query: float32 [1024, 1024], P(None, 'tensor')
- d_w_key: float32 [1024, 512], P(None, 'tensor')
- d_w_value: float32 [1024, 512], P(None, 'tensor')
- d_w_output: float32 [1024, 1024], P('tensor')
- d_norm2_gain: float32 [1024], replicated
- d_w_gate: float32 [32, 1024, 512], P('dp', None, 'tensor')
- d_w_up: float32 [32, 1024, 512], P('dp', None, 'tensor')
- d_w_down: float32 [32, 512, 1024], P('dp', 'tensor')
The draws below stay inside these ranges and needn't reach their ends.
Inputs may be any that keep to these rules, and one draw needn't show every extreme that they name: `seq_lengths`: each index of dp has 3 sequences whose lengths sum to 256; on every index the longest is exactly 224. `routes`: each row names 8 different experts. Among the 256 rows of one index of dp no expert is named more than 80 times, and in every draw some index names some expert exactly 80 times. `gates`: each row is positive and sums to one.
All inputs are finite; a program needn't handle non-finite values.
Results may differ from the reference program's by a relative error of at most 0.015.
Values may be sent and summed in bfloat16 or wider, within the bound.
A program may use at most 192 MiB of HBM per device.

```python
import math
import jax
import jax.numpy as jnp
import numpy as np
from jax import lax

MODEL_WIDTH = 1024
QUERY_HEAD_COUNT = 16
KEY_VALUE_HEADS = 8
HEAD_SIZE = 64
FF = 512
EXPERTS = 32
TOPK = 8
SHARD_TOKENS = 256
SEQS = 3
LONGEST = 224
SLOT = 80
TOKENS = 2048
N_DP = 8


def draw_gates(key, part):
    logits = 0.5 * jax.random.normal(key, (TOKENS, TOPK), jnp.float32)
    return jax.nn.softmax(logits, axis=-1)


def levels(own_key, extent, cuts, smallest, top_value):
    def one(dim, shards_of):
        steps = jax.random.uniform(jax.random.fold_in(jax.random.fold_in(own_key, 6), dim), (shards_of,), jnp.float32, smallest / len(cuts), top_value / len(cuts))
        return jnp.repeat(jnp.exp(steps), extent[dim] // shards_of).reshape((-1,) + (1,) * (len(extent) - dim - 1))

    gain = one(*cuts[0])
    for cut in cuts[1:]:
        gain = gain * one(*cut)
    return gain


def split_up(number_of, total, bound, skew):
    loads = [(1 << 20) // math.isqrt(rank ** skew) + 1 for rank in range(2, number_of + 1)]
    surplus, counts = total - bound - (number_of - 1), [1] * (number_of - 1)
    while surplus > 0:
        candidates = [i for i in range(number_of - 1) if counts[i] < bound]
        mass, budget = sum([loads[i] for i in candidates]), surplus
        for i in candidates:
            addition = min(bound - counts[i], max(1, budget * loads[i] // mass), surplus)
            counts[i] = counts[i] + addition
            surplus = surplus - addition
    return np.array([bound] + counts)


def uneven_parts(stream_key, number_of, total, most, lean):
    if number_of == 2:
        one = jax.random.randint(stream_key, (), max(1, total - most), min(most, total - 1) + 1)
        return jnp.stack([one, total - one])
    tallies = jnp.asarray(split_up(number_of, total, most, lean), jnp.int32)
    couples = (number_of - 1) // 2
    source_of, sink = tallies[1:1 + 2 * couples:2], tallies[2:2 + 2 * couples:2]
    margin = jnp.minimum(source_of - 1, most - sink)
    shifted = jax.random.randint(jax.random.fold_in(stream_key, 1), (couples,), 0, 1 << 20) % (margin + 1)
    tallies = tallies.at[1:1 + 2 * couples:2].set(source_of - shifted).at[2:2 + 2 * couples:2].set(sink + shifted)
    return tallies[jax.random.permutation(jax.random.fold_in(stream_key, 2), number_of)]


def deal_out(own_key, own, number, rows, count, top, most, skew):
    sequence = jax.random.permutation(own_key, count)
    heavy_load, usual = load_shares(count, rows * top, most, skew, True), load_shares(count, rows * top, most, skew, False)
    places = jnp.arange(count)

    def named(tallies, offset_by):
        used = int((tallies > 0).sum())
        fixed = max(1, used // 4)
        passed = fixed + (places - fixed + offset_by * (used - fixed)) % max(1, count - fixed)
        return jnp.zeros((count,), jnp.int32).at[sequence[jnp.where(places < fixed, places, passed)]].set(jnp.asarray(tallies, jnp.int32))

    tallies = jnp.where(number % 4 == 0, named(heavy_load, number // 4), named(usual, number - number // 4 - 1))
    mixed = jax.random.permutation(jax.random.fold_in(own, 3), count)
    giver, sink = mixed[0:count // 2 * 2:2], mixed[1:count // 2 * 2:2]
    margin = jnp.minimum(tallies[giver] - 1, most - tallies[sink]) // 2
    margin = jnp.where((giver == sequence[0]) | (sink == sequence[0]) | (tallies[sink] == 0), 0, jnp.maximum(margin, 0))
    passed = jax.random.randint(jax.random.fold_in(own, 4), (count // 2,), 0, 1 << 20) % (margin + 1)
    tallies = tallies.at[giver].add(-passed).at[sink].add(passed)
    labels = jnp.searchsorted(jnp.cumsum(tallies), jnp.arange(rows * top), side="right").astype(jnp.int32)
    table = labels.reshape(top, rows).T
    table = table[jax.random.permutation(jax.random.fold_in(own, 1), rows)]
    offset_by = jax.random.randint(jax.random.fold_in(own, 2), (rows, 1), 0, top)
    return jnp.take_along_axis(table, (jnp.arange(top)[None, :] + offset_by) % top, axis=1)


def load_shares(number_of, total, limit, skew, full):
    loads = [(1 << 20) // math.isqrt(grade ** skew) + 1 for grade in range(1, number_of + 1)]
    largest = limit if full else min(limit, max(-(-total // number_of), total * loads[0] // sum(loads)))
    least = 1 if total - largest >= number_of - 1 else 0
    given, surplus = [largest] + [least] * (number_of - 1), total - largest - least * (number_of - 1)
    while surplus > 0:
        movable = [i for i in range(1, number_of) if given[i] < largest] or [i for i in range(1, number_of) if given[i] < limit]
        whole, left = sum([loads[i] for i in movable]), surplus
        for i in movable:
            more = min(limit - given[i], max(1, left * loads[i] // whole), surplus)
            given[i] = given[i] + more
            surplus = surplus - more
    return np.array(given)


def scatter_about(rng, shape, scale, reach, split=(), kind=jnp.bfloat16):
    factor_of = levels(rng, shape, split, -0.22, 0.18) if split else 1.0
    drawn = jax.random.normal(rng, shape, jnp.float32) * scale * factor_of
    return jnp.minimum(jnp.maximum(drawn, -reach), reach).astype(kind)


def setup_inputs(seed: int = 0) -> dict:
    streams_of = jax.random.split(jax.random.key(seed), 15)
    tokens = scatter_about(streams_of[0], (TOKENS, MODEL_WIDTH), 1.0, 6.0, ((0, 8),))
    cotangent = scatter_about(streams_of[1], (TOKENS, MODEL_WIDTH), 1.0, 6.0, ((0, 8),))
    seq_lengths = jax.vmap(lambda own: uneven_parts(own, SEQS, SHARD_TOKENS, LONGEST, 1))(jax.random.split(streams_of[2], N_DP)).reshape((N_DP, SEQS)).astype(jnp.int32)
    routes_keys = jax.random.split(jax.random.fold_in(streams_of[3], 1), TOKENS // SHARD_TOKENS)
    routes_turns = jax.random.permutation(jax.random.fold_in(streams_of[3], 3), TOKENS // SHARD_TOKENS)
    routes = jax.vmap(lambda own, number: deal_out(jax.random.fold_in(streams_of[3], 2), own, number, SHARD_TOKENS, EXPERTS, TOPK, SLOT, 1))(routes_keys, routes_turns).reshape((TOKENS, TOPK))
    gates = draw_gates(jax.random.fold_in(streams_of[14], 71), 0)
    norm1_gain = jnp.clip(1.0 + 0.1 * jax.random.normal(streams_of[5], (MODEL_WIDTH,), jnp.float32), 0.5, 1.5)
    w_query = scatter_about(streams_of[6], (MODEL_WIDTH, QUERY_HEAD_COUNT * HEAD_SIZE), MODEL_WIDTH ** -0.5, 0.1875, ((1, 4),))
    key_weight = scatter_about(streams_of[7], (MODEL_WIDTH, KEY_VALUE_HEADS * HEAD_SIZE), MODEL_WIDTH ** -0.5, 0.1875, ((1, 4),))
    value_weight = scatter_about(streams_of[8], (MODEL_WIDTH, KEY_VALUE_HEADS * HEAD_SIZE), MODEL_WIDTH ** -0.5, 0.1875, ((1, 4),))
    w_output = scatter_about(streams_of[9], (QUERY_HEAD_COUNT * HEAD_SIZE, MODEL_WIDTH), (QUERY_HEAD_COUNT * HEAD_SIZE // 16) ** -0.5, 0.75, ((0, 4),))
    norm2_gain = jnp.clip(1.0 + 0.1 * jax.random.normal(streams_of[10], (MODEL_WIDTH,), jnp.float32), 0.5, 1.5)
    w_gate = scatter_about(streams_of[11], (EXPERTS, MODEL_WIDTH, FF), MODEL_WIDTH ** -0.5, 0.1875, ((0, 8), (2, 4)))
    w_up = scatter_about(streams_of[12], (EXPERTS, MODEL_WIDTH, FF), MODEL_WIDTH ** -0.5, 0.1875, ((0, 8), (2, 4)))
    w_down = scatter_about(streams_of[13], (EXPERTS, FF, MODEL_WIDTH), (FF // 16) ** -0.5, 1.0, ((0, 8), (1, 4)))
    return dict(tokens=tokens, cotangent=cotangent, seq_lengths=seq_lengths, routes=routes, gates=gates, norm1_gain=norm1_gain, w_query=w_query, key_weight=key_weight, value_weight=value_weight, w_output=w_output, norm2_gain=norm2_gain, w_gate=w_gate, w_up=w_up, w_down=w_down)


EPSILON = 1e-05
ROPE_BASE = 10000.0
EXACT_PRECISION = lax.Precision.HIGHEST

@jax.custom_vjp
def reduced_dtype(v):
    return lax.optimization_barrier(v.astype(jnp.bfloat16)).astype(jnp.float32)

@jax.custom_vjp
def reduced_backward(v):
    return v

def low_keep(v):
    return (reduced_dtype(v), None)

def low_pass(kept, grad):
    return (grad,)

def back_keep(v):
    return (v, None)

def back_low(kept, grad):
    return (reduced_dtype(grad),)
reduced_dtype.defvjp(low_keep, low_pass)
reduced_backward.defvjp(back_keep, back_low)

def layout(lengths, row_total):
    seq_ends = jnp.cumsum(lengths).astype(jnp.int32)
    seq_starts = (seq_ends - lengths).astype(jnp.int32)
    row_ids = jnp.arange(row_total, dtype=jnp.int32)
    segment = lax.optimization_barrier(jnp.sum((row_ids[:, None] >= seq_ends[None, :]).astype(jnp.int32), axis=1)).astype(jnp.int32)
    member = segment[:, None] == jnp.arange(lengths.shape[0], dtype=jnp.int32)[None, :]
    seq_begin = lax.optimization_barrier(jnp.sum(jnp.where(member, seq_starts[None, :], 0), axis=1)).astype(jnp.int32)
    position = row_ids - seq_begin
    allowed = (segment[:, None] == segment[None, :]) & (row_ids[None, :] <= row_ids[:, None])
    return (position, allowed)

def rotary(position, width):
    half_width = width // 2
    frequency = ROPE_BASE ** (-2.0 * jnp.arange(half_width, dtype=jnp.float32) / width)
    angles = position.astype(jnp.float32)[:, None] * frequency[None, :]
    return (jnp.cos(angles), jnp.sin(angles))

def apply_rotation(rows_three, cosine_table, sine_table):
    half_width = rows_three.shape[-1] // 2
    first_half = rows_three[..., :half_width]
    second_half = rows_three[..., half_width:]
    cos_rows = cosine_table[:, None, :]
    sin_rows = sine_table[:, None, :]
    return jnp.concatenate([first_half * cos_rows - second_half * sin_rows, second_half * cos_rows + first_half * sin_rows], axis=-1)

def slot_table(routes):
    flat_routes = routes.reshape(-1).astype(jnp.int32)
    onehot = (flat_routes[:, None] == jnp.arange(EXPERTS, dtype=jnp.int32)[None, :]).astype(jnp.int32)
    before = jnp.cumsum(onehot, axis=0).astype(jnp.int32) - onehot
    rank_in = lax.optimization_barrier(jnp.sum(before * onehot, axis=1)).astype(jnp.int32)
    return (flat_routes * SLOT + rank_in).astype(jnp.int32)

def rms_norm(values, gain_vec):
    inv_rms = lax.rsqrt(lax.optimization_barrier(jnp.mean(values * values, axis=-1, keepdims=True)) + EPSILON)
    return values * inv_rms * gain_vec

def block_forward(weights, inputs):
    norm1_gain, w_query, key_weight, value_weight, w_output, norm2_gain, w_gate, w_up, w_down = weights
    tokens, lengths, routes, gates = inputs
    position, allowed = layout(lengths, SHARD_TOKENS)
    cosine_table, sine_table = rotary(position, HEAD_SIZE)
    head_group = QUERY_HEAD_COUNT // KEY_VALUE_HEADS
    normalized_input = reduced_dtype(rms_norm(tokens, norm1_gain))
    query_unrotated = reduced_backward(jnp.dot(normalized_input, w_query, precision=EXACT_PRECISION)).reshape(SHARD_TOKENS, QUERY_HEAD_COUNT, HEAD_SIZE)
    query_matrix = reduced_dtype(apply_rotation(query_unrotated, cosine_table, sine_table)).reshape(SHARD_TOKENS, KEY_VALUE_HEADS, head_group, HEAD_SIZE)
    key_unrotated = reduced_backward(jnp.dot(normalized_input, key_weight, precision=EXACT_PRECISION)).reshape(SHARD_TOKENS, KEY_VALUE_HEADS, HEAD_SIZE)
    key_rows = reduced_dtype(apply_rotation(key_unrotated, cosine_table, sine_table))
    value_matrix = reduced_dtype(reduced_backward(jnp.dot(normalized_input, value_weight, precision=EXACT_PRECISION))).reshape(SHARD_TOKENS, KEY_VALUE_HEADS, HEAD_SIZE)
    scores = reduced_backward(jnp.einsum('qkgd,skd->kgqs', query_matrix, key_rows, precision=EXACT_PRECISION) * HEAD_SIZE ** (-0.5))
    scores = jnp.where(allowed[None, None], scores, -1000000000.0)
    top_score = lax.optimization_barrier(jnp.max(scores, axis=-1, keepdims=True))
    exponent = jnp.exp(scores - top_score)
    prob_low = reduced_dtype(exponent / lax.optimization_barrier(jnp.sum(exponent, axis=-1, keepdims=True)))
    mixed_heads = jnp.einsum('kgqs,skd->qkgd', prob_low, value_matrix, precision=EXACT_PRECISION).reshape(SHARD_TOKENS, QUERY_HEAD_COUNT * HEAD_SIZE)
    mixed_heads = reduced_dtype(reduced_backward(mixed_heads))
    attended = reduced_backward(jnp.dot(mixed_heads, w_output, precision=EXACT_PRECISION))
    hidden = tokens + attended
    normed2 = reduced_dtype(rms_norm(hidden, norm2_gain))
    place = slot_table(routes)
    route_token = jnp.arange(SHARD_TOKENS * TOPK, dtype=jnp.int32) // TOPK
    source = jnp.zeros((EXPERTS * SLOT,), jnp.int32).at[place].set(route_token)
    occupied = jnp.zeros((EXPERTS * SLOT,), jnp.float32).at[place].set(1.0)
    slot_rows = reduced_backward(normed2[source] * occupied[:, None]).reshape(EXPERTS, SLOT, MODEL_WIDTH)
    gate_pre = reduced_backward(jnp.einsum('esd,edf->esf', slot_rows, w_gate, precision=EXACT_PRECISION))
    up_pre = reduced_backward(jnp.einsum('esd,edf->esf', slot_rows, w_up, precision=EXACT_PRECISION))
    activated = reduced_dtype(jax.nn.silu(gate_pre) * up_pre)
    expert_out = reduced_backward(reduced_dtype(jnp.einsum('esf,efd->esd', activated, w_down, precision=EXACT_PRECISION)))
    routed = expert_out.reshape(EXPERTS * SLOT, MODEL_WIDTH)[place].reshape(SHARD_TOKENS, TOPK, MODEL_WIDTH)
    mixture = lax.optimization_barrier(jnp.sum(gates[:, :, None] * routed, axis=1))
    return hidden + mixture

def reference(tokens, cotangent, seq_lengths, routes, gates, norm1_gain, w_query, key_weight, value_weight, w_output, norm2_gain, w_gate, w_up, w_down):
    floats = [arr.astype(jnp.float32) for arr in (tokens, norm1_gain, w_query, key_weight, value_weight, w_output, norm2_gain, w_gate, w_up, w_down)]
    route_blocks = routes.reshape(N_DP, SHARD_TOKENS, TOPK)
    gate_blocks = gates.astype(jnp.float32).reshape(N_DP, SHARD_TOKENS, TOPK)

    def forward(token_rows, *weights):
        checked = jax.checkpoint(block_forward)

        def one_block(unused_state, inputs):
            return (unused_state, checked(weights, inputs))
        blocks = (token_rows.reshape(N_DP, SHARD_TOKENS, MODEL_WIDTH), seq_lengths, route_blocks, gate_blocks)
        unused_final, outputs = lax.scan(one_block, jnp.zeros((), jnp.float32), blocks)
        return outputs.reshape(TOKENS, MODEL_WIDTH)
    output, pullback = jax.vjp(forward, *floats)
    gradients = pullback(cotangent.astype(jnp.float32))
    return (output.astype(jnp.bfloat16), gradients[0], gradients[1], gradients[2], gradients[3], gradients[4], gradients[5], gradients[6], gradients[7], gradients[8], gradients[9])
```

```python
import jax
import jax.numpy as jnp
from jax import lax
from jax.experimental import pallas as pl
from jax.experimental.pallas import tpu as pltpu
from jax.sharding import PartitionSpec as P

HEAD_SIZE = 64
EXPERTS = 32
LANES = 128
TILE = 512


EPSILON = 1e-05
ROPE_BASE = 10000.0


def layout(lengths, row_total):
    order = jnp.arange(lengths.shape[0], dtype=jnp.int32)
    seq_ends = jnp.sum(jnp.where(order[None, :] <= order[:, None], lengths[None, :], 0), axis=1)
    seq_starts = seq_ends - lengths
    row_ids = jnp.arange(row_total, dtype=jnp.int32)
    segment = jnp.sum((row_ids[:, None] >= seq_ends[None, :]).astype(jnp.int32), axis=1)
    member = segment[:, None] == jnp.arange(lengths.shape[0], dtype=jnp.int32)[None, :]
    seq_begin = jnp.sum(jnp.where(member, seq_starts[None, :], 0), axis=1)
    position = row_ids - seq_begin
    allowed = (segment[:, None] == segment[None, :]) & (row_ids[None, :] <= row_ids[:, None])
    return (position, allowed)


def rotary(position, width):
    half_width = width // 2
    frequency = ROPE_BASE ** (-2.0 * jnp.arange(half_width, dtype=jnp.float32) / width)
    angles = position.astype(jnp.float32)[:, None] * frequency[None, :]
    return (jnp.cos(angles), jnp.sin(angles))


def apply_rotation(rows_three, cosine_table, sine_table):
    half_width = rows_three.shape[-1] // 2
    first_half = rows_three[..., :half_width]
    second_half = rows_three[..., half_width:]
    cos_rows = cosine_table[:, None, :]
    sin_rows = sine_table[:, None, :]
    return jnp.concatenate(
        [
            first_half * cos_rows - second_half * sin_rows,
            second_half * cos_rows + first_half * sin_rows,
        ],
        axis=-1,
    )


def norm_back(grad_out, unit_rows, inv_rms, gain_vec):
    scaled = grad_out * gain_vec
    return inv_rms * (scaled - unit_rows * jnp.mean(scaled * unit_rows, axis=-1, keepdims=True))


def dot(left, right, left_dim, right_dim):
    return lax.dot_general(
        left,
        right,
        (((left_dim,), (right_dim,)), ((), ())),
        preferred_element_type=jnp.float32,
    )


def expert_kernel(
    rows_ref,
    cot_ref,
    gate_ref,
    pick_ref,
    w_gate_ref,
    w_up_ref,
    w_down_ref,
    mix_ref,
    grad_ref,
    d_gate_ref,
    d_up_ref,
    d_down_ref,
    weights,
    total,
):
    step = pl.program_id(0)
    experts, _, hidden_units = w_gate_ref.shape
    units = experts * hidden_units

    @pl.when(step == 0)
    def _():
        for e in range(experts):
            weights[:, e * hidden_units : (e + 1) * hidden_units] = w_gate_ref[e]
            weights[:, units + e * hidden_units : units + (e + 1) * hidden_units] = w_up_ref[e]
        total[...] = jnp.zeros_like(total)
        d_down_ref[...] = jnp.zeros_like(d_down_ref)

    rows = rows_ref[...]
    cot = cot_ref[...]
    gate = dot(gate_ref[...], pick_ref[...], 1, 0)
    gate_pre = dot(rows, weights[:, :units], 1, 0)
    up_pre = dot(rows, weights[:, units:], 1, 0)
    sigmoid_gate = jax.nn.sigmoid(gate_pre)
    swish = gate_pre * sigmoid_gate
    slope = sigmoid_gate * (1.0 + gate_pre * (1.0 - sigmoid_gate))
    activated = (swish * up_pre * gate).astype(jnp.bfloat16)
    grad_act = dot(cot, w_down_ref[...], 1, 1) * gate
    grad_gate = (grad_act * up_pre * slope).astype(jnp.bfloat16)
    grad_up = (grad_act * swish).astype(jnp.bfloat16)
    grad_rows = dot(grad_gate, weights[:, :units], 1, 1) + dot(grad_up, weights[:, units:], 1, 1)
    grad_ref[...] = grad_rows.astype(jnp.bfloat16)
    mix_ref[...] = dot(activated, w_down_ref[...], 1, 0).astype(jnp.bfloat16)
    total[:, :units] += dot(rows, grad_gate, 0, 0)
    total[:, units:] += dot(rows, grad_up, 0, 0)
    d_down_ref[...] += dot(activated, cot, 0, 0)

    @pl.when(step == pl.num_programs(0) - 1)
    def _():
        for e in range(experts):
            d_gate_ref[e] = total[:, e * hidden_units : (e + 1) * hidden_units]
            d_up_ref[e] = total[:, units + e * hidden_units : units + (e + 1) * hidden_units]


def experts_both_ways(rows, cot_gates, pick, w_gate, w_up, w_down):
    row_total, width = rows.shape
    experts, _, hidden_units = w_gate.shape
    units = experts * hidden_units
    tile = min(TILE, row_total)
    tiled = pl.BlockSpec((tile, width), lambda i: (i, 0))
    flat = pl.BlockSpec((units, width), lambda i: (0, 0))
    deep = pl.BlockSpec((experts, width, hidden_units), lambda i: (0, 0, 0))
    return pl.pallas_call(
        expert_kernel,
        grid=(row_total // tile,),
        in_specs=[
            tiled,
            tiled,
            pl.BlockSpec((tile, LANES), lambda i: (i, width // LANES)),
            pl.BlockSpec((LANES, units), lambda i: (0, 0)),
            deep,
            deep,
            flat,
        ],
        out_specs=[tiled, tiled, deep, deep, flat],
        out_shape=[
            jax.ShapeDtypeStruct((row_total, width), jnp.bfloat16),
            jax.ShapeDtypeStruct((row_total, width), jnp.bfloat16),
            jax.ShapeDtypeStruct(w_gate.shape, jnp.float32),
            jax.ShapeDtypeStruct(w_up.shape, jnp.float32),
            jax.ShapeDtypeStruct((units, width), jnp.float32),
        ],
        scratch_shapes=[
            pltpu.VMEM((width, 2 * units), jnp.bfloat16),
            pltpu.VMEM((width, 2 * units), jnp.float32),
        ],
        compiler_params=pltpu.CompilerParams(vmem_limit_bytes=56 * 2**20),
        cost_estimate=pl.CostEstimate(
            flops=18 * row_total * width * units,
            bytes_accessed=8 * row_total * width + 18 * width * units,
            transcendentals=row_total * units,
        ),
    )(rows, cot_gates, cot_gates, pick, w_gate, w_up, w_down.reshape(units, width))


def body(
    tokens,
    cotangent,
    seq_lengths,
    routes,
    gates,
    norm1_gain,
    w_query,
    key_weight,
    value_weight,
    w_output,
    norm2_gain,
    w_gate,
    w_up,
    w_down,
):
    rows_count, width = tokens.shape
    query_heads = w_query.shape[1] // HEAD_SIZE
    kv_heads = key_weight.shape[1] // HEAD_SIZE
    head_group = query_heads // kv_heads
    local_experts, _, hidden_units = w_gate.shape
    members = lax.axis_size("tensor")
    member_id = lax.axis_index("tensor")
    quarter = rows_count // members
    score_scale = HEAD_SIZE ** (-0.5)
    everyone = ("dp", "tensor")

    def own(rows):
        return lax.dynamic_slice_in_dim(rows, member_id * quarter, quarter, 0)

    def scatter(rows, axes):
        return lax.psum_scatter(
            rows.astype(jnp.bfloat16), axes, scatter_dimension=0, tiled=True
        ).astype(jnp.float32)

    def gather(rows, axes):
        return lax.all_gather(rows.astype(jnp.bfloat16), axes, axis=0, tiled=True)

    expert_ids = jnp.arange(EXPERTS, dtype=jnp.int32)
    gate_dense = jnp.sum(
        jnp.where(own(routes)[:, :, None] == expert_ids, own(gates)[:, :, None], 0.0), axis=1
    )
    gate_high = gate_dense.astype(jnp.bfloat16)
    gate_low = (gate_dense - gate_high.astype(jnp.float32)).astype(jnp.bfloat16)
    blank = jnp.zeros((quarter, LANES - 2 * EXPERTS), jnp.bfloat16)
    own_cot = own(cotangent)
    cot_gates = gather(
        jnp.concatenate([own_cot, gate_high, gate_low, blank], axis=1), everyone
    )
    first_expert = lax.axis_index("dp") * local_experts
    column_expert = first_expert + jnp.arange(local_experts * hidden_units) // hidden_units
    lane = jnp.arange(LANES, dtype=jnp.int32)
    pick = (
        (lane[:, None] % EXPERTS == column_expert[None, :]) & (lane[:, None] < 2 * EXPERTS)
    ).astype(jnp.bfloat16)

    position, allowed = layout(seq_lengths.reshape(-1), rows_count)
    cosine_table, sine_table = rotary(position, HEAD_SIZE)
    inputs = tokens.astype(jnp.float32)
    inv_rms1 = lax.rsqrt(jnp.mean(inputs * inputs, axis=-1, keepdims=True) + EPSILON)
    unit1 = inputs * inv_rms1
    normalized_input = (unit1 * norm1_gain).astype(jnp.bfloat16)
    qkv_weight = jnp.concatenate([w_query, key_weight, value_weight], axis=1)
    query_width = query_heads * HEAD_SIZE
    kv_width = kv_heads * HEAD_SIZE
    qkv = jnp.dot(normalized_input, qkv_weight, preferred_element_type=jnp.float32)
    query_unrotated = qkv[:, :query_width].reshape(rows_count, query_heads, HEAD_SIZE)
    key_unrotated = qkv[:, query_width : query_width + kv_width].reshape(
        rows_count, kv_heads, HEAD_SIZE
    )
    query_matrix = (
        apply_rotation(query_unrotated, cosine_table, sine_table)
        .astype(jnp.bfloat16)
        .reshape(rows_count, kv_heads, head_group, HEAD_SIZE)
    )
    key_rows = apply_rotation(key_unrotated, cosine_table, sine_table).astype(jnp.bfloat16)
    value_matrix = (
        qkv[:, query_width + kv_width :]
        .astype(jnp.bfloat16)
        .reshape(rows_count, kv_heads, HEAD_SIZE)
    )
    raw_scores = (
        jnp.einsum("qkgd,skd->kgqs", query_matrix, key_rows, preferred_element_type=jnp.float32)
        * score_scale
    )
    scores = jnp.where(allowed, raw_scores, -1000000000.0)
    top_score = jnp.max(scores, axis=-1, keepdims=True)
    exponent = jnp.exp(scores - top_score)
    denominator = jnp.sum(exponent, axis=-1, keepdims=True)
    prob_full = exponent / denominator
    prob_low = prob_full.astype(jnp.bfloat16)
    mixed_heads = jnp.einsum(
        "kgqs,skd->qkgd", prob_low, value_matrix, preferred_element_type=jnp.float32
    )
    mixed_heads = mixed_heads.reshape(rows_count, query_width).astype(jnp.bfloat16)
    attended = scatter(
        jnp.dot(mixed_heads, w_output, preferred_element_type=jnp.float32), "tensor"
    )
    hidden = own(inputs) + attended
    inv_rms2 = lax.rsqrt(jnp.mean(hidden * hidden, axis=-1, keepdims=True) + EPSILON)
    unit2 = hidden * inv_rms2
    normed2 = gather(unit2 * norm2_gain, everyone)
    partial_mix, partial_grad, d_gate, d_up, d_down = experts_both_ways(
        normed2, cot_gates, pick, w_gate, w_up, w_down
    )
    grad_norm2 = scatter(partial_grad, everyone)
    mixture = scatter(partial_mix, everyone)
    result = gather(hidden + mixture, "tensor")
    grad_hidden = own_cot.astype(jnp.float32) + norm_back(grad_norm2, unit2, inv_rms2, norm2_gain)
    d_norm2 = jnp.sum(grad_norm2 * unit2, axis=0)
    grad_attended = gather(grad_hidden, "tensor")
    d_output = jnp.einsum(
        "rh,rd->hd", mixed_heads, grad_attended, preferred_element_type=jnp.float32
    )
    d_output = lax.psum(d_output.astype(jnp.bfloat16), "dp").astype(jnp.float32)
    grad_mixed = jnp.einsum(
        "rd,hd->rh", grad_attended, w_output, preferred_element_type=jnp.float32
    )
    grad_mixed = grad_mixed.astype(jnp.bfloat16).reshape(
        rows_count, kv_heads, head_group, HEAD_SIZE
    )
    grad_probs = jnp.einsum(
        "qkgd,skd->kgqs", grad_mixed, value_matrix, preferred_element_type=jnp.float32
    )
    grad_values = jnp.einsum(
        "kgqs,qkgd->skd", prob_low, grad_mixed, preferred_element_type=jnp.float32
    )
    grad_values = grad_values.astype(jnp.bfloat16).reshape(rows_count, kv_width)
    inner_sum = jnp.sum(grad_probs * prob_full, axis=-1, keepdims=True)
    grad_scores = (prob_full * (grad_probs - inner_sum)).astype(jnp.bfloat16)
    grad_queries = (
        jnp.einsum("kgqs,skd->qkgd", grad_scores, key_rows, preferred_element_type=jnp.float32)
        * score_scale
    )
    grad_keys = (
        jnp.einsum("kgqs,qkgd->skd", grad_scores, query_matrix, preferred_element_type=jnp.float32)
        * score_scale
    )
    grad_qpre = apply_rotation(
        grad_queries.reshape(rows_count, query_heads, HEAD_SIZE), cosine_table, -sine_table
    )
    grad_qpre = grad_qpre.astype(jnp.bfloat16).reshape(rows_count, query_width)
    grad_kpre = (
        apply_rotation(grad_keys, cosine_table, -sine_table)
        .astype(jnp.bfloat16)
        .reshape(rows_count, kv_width)
    )
    grad_qkv = jnp.concatenate([grad_qpre, grad_kpre, grad_values], axis=1)
    d_qkv = jnp.einsum("rd,rf->df", normalized_input, grad_qkv, preferred_element_type=jnp.float32)
    d_qkv = lax.psum(d_qkv.astype(jnp.bfloat16), "dp").astype(jnp.float32)
    grad_normed = jnp.einsum("rf,df->rd", grad_qkv, qkv_weight, preferred_element_type=jnp.float32)
    d_norms = lax.psum(jnp.stack([jnp.sum(grad_normed * unit1, axis=0), d_norm2]), everyone)
    grad_norm1 = scatter(grad_normed, "tensor")
    grad_tokens = grad_hidden + norm_back(grad_norm1, own(unit1), own(inv_rms1), norm1_gain)
    return (
        result,
        gather(grad_tokens, "tensor").astype(jnp.float32),
        d_norms[0],
        d_qkv[:, :query_width],
        d_qkv[:, query_width : query_width + kv_width],
        d_qkv[:, query_width + kv_width :],
        d_output,
        d_norms[1],
        d_gate,
        d_up,
        d_down.reshape(w_down.shape),
    )


def solution(mesh):
    in_specs = (
        P("dp", None),
        P("dp", None),
        P("dp", None),
        P("dp", None),
        P("dp", None),
        P(),
        P(None, "tensor"),
        P(None, "tensor"),
        P(None, "tensor"),
        P("tensor", None),
        P(),
        P("dp", None, "tensor"),
        P("dp", None, "tensor"),
        P("dp", "tensor", None),
    )
    out_specs = (
        P("dp", None),
        P("dp", None),
        P(),
        P(None, "tensor"),
        P(None, "tensor"),
        P(None, "tensor"),
        P("tensor", None),
        P(),
        P("dp", None, "tensor"),
        P("dp", None, "tensor"),
        P("dp", "tensor", None),
    )
    return jax.shard_map(body, mesh=mesh, in_specs=in_specs, out_specs=out_specs, check_vma=False)
```

```python
import functools

import jax
import jax.numpy as jnp
from jax import lax
from jax.experimental import pallas as pl
from jax.experimental.pallas import tpu as pltpu
from jax.sharding import PartitionSpec as P

HEAD_SIZE = 64
EXPERTS = 32
LANES = 128
TILE = 512


EPSILON = 1e-05
ROPE_BASE = 10000.0


def layout(lengths, row_total):
    order = jnp.arange(lengths.shape[0], dtype=jnp.int32)
    seq_ends = jnp.sum(jnp.where(order[None, :] <= order[:, None], lengths[None, :], 0), axis=1)
    seq_starts = seq_ends - lengths
    row_ids = jnp.arange(row_total, dtype=jnp.int32)
    segment = jnp.sum((row_ids[:, None] >= seq_ends[None, :]).astype(jnp.int32), axis=1)
    member = segment[:, None] == jnp.arange(lengths.shape[0], dtype=jnp.int32)[None, :]
    seq_begin = jnp.sum(jnp.where(member, seq_starts[None, :], 0), axis=1)
    position = row_ids - seq_begin
    allowed = (segment[:, None] == segment[None, :]) & (row_ids[None, :] <= row_ids[:, None])
    return (position, allowed)


def rotary(position, width):
    half_width = width // 2
    frequency = ROPE_BASE ** (-2.0 * jnp.arange(half_width, dtype=jnp.float32) / width)
    angles = position.astype(jnp.float32)[:, None] * frequency[None, :]
    return (jnp.cos(angles), jnp.sin(angles))


def apply_rotation(rows_three, cosine_table, sine_table):
    half_width = rows_three.shape[-1] // 2
    first_half = rows_three[..., :half_width]
    second_half = rows_three[..., half_width:]
    cos_rows = cosine_table[:, None, :]
    sin_rows = sine_table[:, None, :]
    return jnp.concatenate(
        [
            first_half * cos_rows - second_half * sin_rows,
            second_half * cos_rows + first_half * sin_rows,
        ],
        axis=-1,
    )


def norm_back(grad_out, unit_rows, inv_rms, gain_vec):
    scaled = grad_out * gain_vec
    return inv_rms * (scaled - unit_rows * jnp.mean(scaled * unit_rows, axis=-1, keepdims=True))


def dot(left, right, left_dim, right_dim):
    return lax.dot_general(
        left,
        right,
        (((left_dim,), (right_dim,)), ((), ())),
        preferred_element_type=jnp.float32,
    )


def expert_kernel(
    quarter,
    rows_ref,
    cot_ref,
    gate_ref,
    pick_ref,
    w_gate_ref,
    w_up_ref,
    w_down_ref,
    mix_ref,
    grad_ref,
    d_gate_ref,
    d_up_ref,
    d_down_ref,
    weights,
    total,
):
    step = pl.program_id(0)
    experts, _, hidden_units = w_gate_ref.shape
    units = experts * hidden_units

    @pl.when(step == 0)
    def _():
        for e in range(experts):
            weights[:, e * hidden_units : (e + 1) * hidden_units] = w_gate_ref[e]
            weights[:, units + e * hidden_units : units + (e + 1) * hidden_units] = w_up_ref[e]
        total[...] = jnp.zeros_like(total)
        d_down_ref[...] = jnp.zeros_like(d_down_ref)

    rows = rows_ref[...]
    cot = cot_ref[...]
    gate = dot(gate_ref[...], pick_ref[...], 1, 0)
    gate_pre = dot(rows, weights[:, :units], 1, 0)
    up_pre = dot(rows, weights[:, units:], 1, 0)
    sigmoid_gate = jax.nn.sigmoid(gate_pre)
    swish = gate_pre * sigmoid_gate
    slope = sigmoid_gate * (1.0 + gate_pre * (1.0 - sigmoid_gate))
    activated = (swish * up_pre * gate).astype(jnp.bfloat16)
    grad_act = dot(cot, w_down_ref[...], 1, 1) * gate
    grad_gate = (grad_act * up_pre * slope).astype(jnp.bfloat16)
    grad_up = (grad_act * swish).astype(jnp.bfloat16)
    grad_rows = dot(grad_gate, weights[:, :units], 1, 1) + dot(grad_up, weights[:, units:], 1, 1)
    grad_rows = grad_rows.astype(jnp.bfloat16)
    mix_rows = dot(activated, w_down_ref[...], 1, 0).astype(jnp.bfloat16)
    members = mix_ref.shape[0]
    for block in range(rows.shape[0] // (members * quarter)):
        here = slice(block * quarter, (block + 1) * quarter)
        for member in range(members):
            first = (block * members + member) * quarter
            grad_ref[member, here] = grad_rows[first : first + quarter]
            mix_ref[member, here] = mix_rows[first : first + quarter]
    total[:, :units] += dot(rows, grad_gate, 0, 0)
    total[:, units:] += dot(rows, grad_up, 0, 0)
    d_down_ref[...] += dot(activated, cot, 0, 0)

    @pl.when(step == pl.num_programs(0) - 1)
    def _():
        for e in range(experts):
            d_gate_ref[e] = total[:, e * hidden_units : (e + 1) * hidden_units]
            d_up_ref[e] = total[:, units + e * hidden_units : units + (e + 1) * hidden_units]


def experts_both_ways(members, quarter, rows, cot_gates, pick, w_gate, w_up, w_down):
    row_total, width = rows.shape
    experts, _, hidden_units = w_gate.shape
    units = experts * hidden_units
    tile = min(TILE, row_total)
    sent = pl.BlockSpec((members, tile // members, width), lambda i: (0, i, 0))
    tiled = pl.BlockSpec((tile, width), lambda i: (i, 0))
    flat = pl.BlockSpec((units, width), lambda i: (0, 0))
    deep = pl.BlockSpec((experts, width, hidden_units), lambda i: (0, 0, 0))
    return pl.pallas_call(
        functools.partial(expert_kernel, quarter),
        grid=(row_total // tile,),
        in_specs=[
            tiled,
            tiled,
            pl.BlockSpec((tile, LANES), lambda i: (i, width // LANES)),
            pl.BlockSpec((LANES, units), lambda i: (0, 0)),
            deep,
            deep,
            flat,
        ],
        out_specs=[sent, sent, deep, deep, flat],
        out_shape=[
            jax.ShapeDtypeStruct((members, row_total // members, width), jnp.bfloat16),
            jax.ShapeDtypeStruct((members, row_total // members, width), jnp.bfloat16),
            jax.ShapeDtypeStruct(w_gate.shape, jnp.float32),
            jax.ShapeDtypeStruct(w_up.shape, jnp.float32),
            jax.ShapeDtypeStruct((units, width), jnp.float32),
        ],
        scratch_shapes=[
            pltpu.VMEM((width, 2 * units), jnp.bfloat16),
            pltpu.VMEM((width, 2 * units), jnp.float32),
        ],
        compiler_params=pltpu.CompilerParams(vmem_limit_bytes=56 * 2**20),
        cost_estimate=pl.CostEstimate(
            flops=18 * row_total * width * units,
            bytes_accessed=8 * row_total * width + 18 * width * units,
            transcendentals=row_total * units,
        ),
    )(rows, cot_gates, cot_gates, pick, w_gate, w_up, w_down.reshape(units, width))


def body(
    tokens,
    cotangent,
    seq_lengths,
    routes,
    gates,
    norm1_gain,
    w_query,
    key_weight,
    value_weight,
    w_output,
    norm2_gain,
    w_gate,
    w_up,
    w_down,
):
    rows_count, width = tokens.shape
    query_heads = w_query.shape[1] // HEAD_SIZE
    kv_heads = key_weight.shape[1] // HEAD_SIZE
    head_group = query_heads // kv_heads
    local_experts, _, hidden_units = w_gate.shape
    sources = lax.axis_size("dp")
    members = lax.axis_size("tensor")
    member_id = lax.axis_index("tensor")
    quarter = rows_count // members
    score_scale = HEAD_SIZE ** (-0.5)
    everyone = ("dp", "tensor")

    def own(rows):
        return lax.dynamic_slice_in_dim(rows, member_id * quarter, quarter, 0)

    def scatter(rows, axes):
        return lax.psum_scatter(
            rows.astype(jnp.bfloat16), axes, scatter_dimension=0, tiled=True
        ).astype(jnp.float32)

    def swap(rows):
        parts = rows.reshape(sources, rows.shape[0] // sources, rows.shape[1])
        parts = lax.all_to_all(parts, "dp", split_axis=0, concat_axis=0, tiled=True)
        return jnp.sum(parts.astype(jnp.float32), axis=0)

    def scatter_all(rows):
        mine = lax.psum_scatter(rows, "tensor", scatter_dimension=0, tiled=True)
        return swap(mine.reshape(rows.shape[1:]))

    def gather(rows, axes):
        return lax.all_gather(rows.astype(jnp.bfloat16), axes, axis=0, tiled=True)

    expert_ids = jnp.arange(EXPERTS, dtype=jnp.int32)
    gate_dense = jnp.sum(
        jnp.where(own(routes)[:, :, None] == expert_ids, own(gates)[:, :, None], 0.0), axis=1
    )
    gate_high = gate_dense.astype(jnp.bfloat16)
    gate_low = (gate_dense - gate_high.astype(jnp.float32)).astype(jnp.bfloat16)
    blank = jnp.zeros((quarter, LANES - 2 * EXPERTS), jnp.bfloat16)
    own_cot = own(cotangent)
    cot_gates = gather(
        jnp.concatenate([own_cot, gate_high, gate_low, blank], axis=1), everyone
    )
    first_expert = lax.axis_index("dp") * local_experts
    column_expert = first_expert + jnp.arange(local_experts * hidden_units) // hidden_units
    lane = jnp.arange(LANES, dtype=jnp.int32)
    pick = (
        (lane[:, None] % EXPERTS == column_expert[None, :]) & (lane[:, None] < 2 * EXPERTS)
    ).astype(jnp.bfloat16)

    position, allowed = layout(seq_lengths.reshape(-1), rows_count)
    cosine_table, sine_table = rotary(position, HEAD_SIZE)
    inputs = tokens.astype(jnp.float32)
    inv_rms1 = lax.rsqrt(jnp.mean(inputs * inputs, axis=-1, keepdims=True) + EPSILON)
    unit1 = inputs * inv_rms1
    normalized_input = (unit1 * norm1_gain).astype(jnp.bfloat16)
    qkv_weight = jnp.concatenate([w_query, key_weight, value_weight], axis=1)
    query_width = query_heads * HEAD_SIZE
    kv_width = kv_heads * HEAD_SIZE
    qkv = jnp.dot(normalized_input, qkv_weight, preferred_element_type=jnp.float32)
    query_unrotated = qkv[:, :query_width].reshape(rows_count, query_heads, HEAD_SIZE)
    key_unrotated = qkv[:, query_width : query_width + kv_width].reshape(
        rows_count, kv_heads, HEAD_SIZE
    )
    query_matrix = (
        apply_rotation(query_unrotated, cosine_table, sine_table)
        .astype(jnp.bfloat16)
        .reshape(rows_count, kv_heads, head_group, HEAD_SIZE)
    )
    key_rows = apply_rotation(key_unrotated, cosine_table, sine_table).astype(jnp.bfloat16)
    value_matrix = (
        qkv[:, query_width + kv_width :]
        .astype(jnp.bfloat16)
        .reshape(rows_count, kv_heads, HEAD_SIZE)
    )
    raw_scores = (
        jnp.einsum("qkgd,skd->kgqs", query_matrix, key_rows, preferred_element_type=jnp.float32)
        * score_scale
    )
    scores = jnp.where(allowed, raw_scores, -1000000000.0)
    top_score = jnp.max(scores, axis=-1, keepdims=True)
    exponent = jnp.exp(scores - top_score)
    denominator = jnp.sum(exponent, axis=-1, keepdims=True)
    prob_full = exponent / denominator
    prob_low = prob_full.astype(jnp.bfloat16)
    mixed_heads = jnp.einsum(
        "kgqs,skd->qkgd", prob_low, value_matrix, preferred_element_type=jnp.float32
    )
    mixed_heads = mixed_heads.reshape(rows_count, query_width).astype(jnp.bfloat16)
    attended = scatter(
        jnp.dot(mixed_heads, w_output, preferred_element_type=jnp.float32), "tensor"
    )
    hidden = own(inputs) + attended
    inv_rms2 = lax.rsqrt(jnp.mean(hidden * hidden, axis=-1, keepdims=True) + EPSILON)
    unit2 = hidden * inv_rms2
    normed2 = gather(unit2 * norm2_gain, everyone)
    partial_mix, partial_grad, d_gate, d_up, d_down = experts_both_ways(
        members, quarter, normed2, cot_gates, pick, w_gate, w_up, w_down
    )
    grad_norm2 = scatter_all(partial_grad)
    mixture = scatter_all(partial_mix)
    result = gather(hidden + mixture, "tensor")
    grad_hidden = own_cot.astype(jnp.float32) + norm_back(grad_norm2, unit2, inv_rms2, norm2_gain)
    d_norm2 = jnp.sum(grad_norm2 * unit2, axis=0)
    grad_attended = gather(grad_hidden, "tensor")
    d_output = jnp.einsum(
        "rh,rd->hd", mixed_heads, grad_attended, preferred_element_type=jnp.float32
    )
    grad_mixed = jnp.einsum(
        "rd,hd->rh", grad_attended, w_output, preferred_element_type=jnp.float32
    )
    grad_mixed = grad_mixed.astype(jnp.bfloat16).reshape(
        rows_count, kv_heads, head_group, HEAD_SIZE
    )
    grad_probs = jnp.einsum(
        "qkgd,skd->kgqs", grad_mixed, value_matrix, preferred_element_type=jnp.float32
    )
    grad_values = jnp.einsum(
        "kgqs,qkgd->skd", prob_low, grad_mixed, preferred_element_type=jnp.float32
    )
    grad_values = grad_values.astype(jnp.bfloat16).reshape(rows_count, kv_width)
    inner_sum = jnp.sum(grad_probs * prob_full, axis=-1, keepdims=True)
    grad_scores = (prob_full * (grad_probs - inner_sum)).astype(jnp.bfloat16)
    grad_queries = (
        jnp.einsum("kgqs,skd->qkgd", grad_scores, key_rows, preferred_element_type=jnp.float32)
        * score_scale
    )
    grad_keys = (
        jnp.einsum("kgqs,qkgd->skd", grad_scores, query_matrix, preferred_element_type=jnp.float32)
        * score_scale
    )
    grad_qpre = apply_rotation(
        grad_queries.reshape(rows_count, query_heads, HEAD_SIZE), cosine_table, -sine_table
    )
    grad_qpre = grad_qpre.astype(jnp.bfloat16).reshape(rows_count, query_width)
    grad_kpre = (
        apply_rotation(grad_keys, cosine_table, -sine_table)
        .astype(jnp.bfloat16)
        .reshape(rows_count, kv_width)
    )
    grad_qkv = jnp.concatenate([grad_qpre, grad_kpre, grad_values], axis=1)
    d_qkv = jnp.einsum("rd,rf->df", normalized_input, grad_qkv, preferred_element_type=jnp.float32)
    d_both = jnp.concatenate(
        [d_qkv.astype(jnp.bfloat16), d_output.astype(jnp.bfloat16).reshape(-1, d_qkv.shape[1])]
    )
    d_both = gather(swap(d_both), "dp").astype(jnp.float32)
    d_qkv = d_both[:width]
    d_output = d_both[width:].reshape(w_output.shape)
    grad_normed = jnp.einsum("rf,df->rd", grad_qkv, qkv_weight, preferred_element_type=jnp.float32)
    d_norms = jnp.stack([jnp.sum(grad_normed * unit1, axis=0), d_norm2])
    d_norms = jnp.sum(lax.all_gather(d_norms, everyone, axis=0), axis=0)
    grad_norm1 = scatter(grad_normed, "tensor")
    grad_tokens = grad_hidden + norm_back(grad_norm1, own(unit1), own(inv_rms1), norm1_gain)
    return (
        result,
        gather(grad_tokens, "tensor").astype(jnp.float32),
        d_norms[0],
        d_qkv[:, :query_width],
        d_qkv[:, query_width : query_width + kv_width],
        d_qkv[:, query_width + kv_width :],
        d_output,
        d_norms[1],
        d_gate,
        d_up,
        d_down.reshape(w_down.shape),
    )


def solution(mesh):
    in_specs = (
        P("dp", None),
        P("dp", None),
        P("dp", None),
        P("dp", None),
        P("dp", None),
        P(),
        P(None, "tensor"),
        P(None, "tensor"),
        P(None, "tensor"),
        P("tensor", None),
        P(),
        P("dp", None, "tensor"),
        P("dp", None, "tensor"),
        P("dp", "tensor", None),
    )
    out_specs = (
        P("dp", None),
        P("dp", None),
        P(),
        P(None, "tensor"),
        P(None, "tensor"),
        P(None, "tensor"),
        P("tensor", None),
        P(),
        P("dp", None, "tensor"),
        P("dp", None, "tensor"),
        P("dp", "tensor", None),
    )
    return jax.shard_map(body, mesh=mesh, in_specs=in_specs, out_specs=out_specs, check_vma=False)
```
